512 devices in a mesh: dp: 32 (over z, x_lo, core), expert: 16 (over x_hi, y).
Axes of the slice: x: 4 (x_hi: 2, x_lo: 2; x = x_hi * 2 + x_lo), y: 8, z: 8, core: 2. Of those that a mesh axis runs over, the one named last changes fastest.
Arguments:
- tokens: bfloat16 [1536, 4096], P(('dp', 'expert')), may hold values from -6 to 6
- expert_ids: int32 [1536, 8], P('dp'), may hold values from 0 to 63, all different within a row; in each aligned block of 48 rows (0 to 47, 48 to 95, ...) at most 10 rows name the same one
- gate_ints: int32 [1536, 8], P('dp'), may hold values from 1024 to 65535
- gate_weight: bfloat16 [512, 192, 4096], P(('expert', 'dp')), may hold values from -0.09375 to 0.09375
- up_weight: bfloat16 [512, 192, 4096], P(('expert', 'dp')), may hold values from -0.09375 to 0.09375
- down_weight: bfloat16 [512, 192, 4096], P(('expert', 'dp')), may hold values from -0.15625 to 0.15625
Outputs:
- mixed: bfloat16 [1536, 4096], P(('dp', 'expert'))
The draws below stay inside these ranges and needn't reach their ends.
Inputs may be any that keep to these rules, and one draw needn't show every extreme that they name: `expert_ids`: each row names 8 different experts. Among the 48 rows of one index of dp (aligned blocks), no expert is named by more than 10 rows, a bound that some block reaches.
All inputs are finite; a program needn't handle non-finite values.
Results may differ from the reference program's by a relative error of at most 0.02.
Values may be sent and summed in bfloat16 or wider, within the bound.
A program may use at most 64 MiB of HBM per device.

```python
import math
import jax
import jax.numpy as jnp
import numpy as np
from jax import lax

D = 4096
FF = 1536
SLICES = 8
TOK_DP = 48
HID = 192
EXPERTS = 64
TOP = 8
MOST = 10
TOKENS = 1536
N_DP = 32


def set_ends(array, rng, least, high):
    place = [jax.random.randint(jax.random.fold_in(rng, axis), (), 0, length) for axis, length in enumerate(array.shape)]
    main_axis = array.shape.index(max(array.shape))
    beside = place[:main_axis] + [(place[main_axis] + 1) % array.shape[main_axis]] + place[main_axis + 1:]
    return array.at[tuple(place)].set(least).at[tuple(beside)].set(high)


def steps_of(key, extent, pieces, smallest, top_value):
    loudness, own = 1.0, jax.random.fold_in(key, 6)
    for dim, blocks in pieces:
        draws = jnp.exp(jax.random.uniform(jax.random.fold_in(own, dim), (blocks,), jnp.float32, smallest / len(pieces), top_value / len(pieces)))
        loudness = loudness * jnp.repeat(draws, extent[dim] // blocks).reshape([-1 if axis == dim else 1 for axis in range(len(extent))])
    return loudness


def shared_out(key, own, number, rows, number_of, top, limit, slope):
    ranking = jax.random.permutation(key, number_of)
    packed, common = portions_of(number_of, rows * top, limit, slope, True), portions_of(number_of, rows * top, limit, slope, False)
    places = jnp.arange(number_of)

    def named(tallies, offset_by):
        used = int((tallies > 0).sum())
        fixed = max(1, used // 4)
        passed = fixed + (places - fixed + offset_by * (used - fixed)) % max(1, number_of - fixed)
        return jnp.zeros((number_of,), jnp.int32).at[ranking[jnp.where(places < fixed, places, passed)]].set(jnp.asarray(tallies, jnp.int32))

    tallies = jnp.where(number % 4 == 0, named(packed, number // 4), named(common, number - number // 4 - 1))
    mixed = jax.random.permutation(jax.random.fold_in(own, 3), number_of)
    donor, taker = mixed[0:number_of // 2 * 2:2], mixed[1:number_of // 2 * 2:2]
    margin = jnp.minimum(tallies[donor] - 1, limit - tallies[taker]) // 2
    margin = jnp.where((donor == ranking[0]) | (taker == ranking[0]) | (tallies[taker] == 0), 0, jnp.maximum(margin, 0))
    passed = jax.random.randint(jax.random.fold_in(own, 4), (number_of // 2,), 0, 1 << 20) % (margin + 1)
    tallies = tallies.at[donor].add(-passed).at[taker].add(passed)
    labels = jnp.searchsorted(jnp.cumsum(tallies), jnp.arange(rows * top), side="right").astype(jnp.int32)
    grid = labels.reshape(top, rows).T
    grid = grid[jax.random.permutation(jax.random.fold_in(own, 1), rows)]
    offset_by = jax.random.randint(jax.random.fold_in(own, 2), (rows, 1), 0, top)
    return jnp.take_along_axis(grid, (jnp.arange(top)[None, :] + offset_by) % top, axis=1)


def portions_of(number_of, total, most, skew, full):
    loads = [(1 << 20) // math.isqrt(grade ** skew) + 1 for grade in range(1, number_of + 1)]
    largest = most if full else min(most, max(-(-total // number_of), total * loads[0] // sum(loads)))
    least = 1 if total - largest >= number_of - 1 else 0
    holding, rest = [largest] + [least] * (number_of - 1), total - largest - least * (number_of - 1)
    while rest > 0:
        candidates = [i for i in range(1, number_of) if holding[i] < largest] or [i for i in range(1, number_of) if holding[i] < most]
        mass, left = sum([loads[i] for i in candidates]), rest
        for i in candidates:
            addition = min(most - holding[i], max(1, left * loads[i] // mass), rest)
            holding[i] = holding[i] + addition
            rest = rest - addition
    return np.array(holding)


def noise(rng, shape, scale, limit, split=(), kind=jnp.bfloat16):
    array = jax.random.normal(rng, shape, jnp.float32) * scale
    if len(split) > 0:
        array = steps_of(rng, shape, split, -0.22, 0.18) * array
    return jnp.clip(array, min=-limit, max=limit).astype(kind)


def setup_inputs(seed: int = 0) -> dict:
    key_of = jax.random.split(jax.random.key(seed), 7)
    tokens = noise(key_of[0], (TOKENS, D), 1.0, 6.0, ((0, 512),))
    expert_ids_keys = jax.random.split(jax.random.fold_in(key_of[1], 1), TOKENS // TOK_DP)
    expert_ids_turns = jax.random.permutation(jax.random.fold_in(key_of[1], 3), TOKENS // TOK_DP)
    expert_ids = jax.vmap(lambda own, number: shared_out(jax.random.fold_in(key_of[1], 2), own, number, TOK_DP, EXPERTS, TOP, MOST, 2))(expert_ids_keys, expert_ids_turns).reshape((TOKENS, TOP))
    gate_ints = set_ends(jax.random.randint(key_of[2], (TOKENS, TOP), 1024, 65536), jax.random.fold_in(key_of[2], 1), 1024, 65535).astype(jnp.int32)
    gate_weight = noise(key_of[3], (EXPERTS * SLICES, HID, D), D ** -0.5, 0.09375, ((0, 512),))
    up_weight = noise(key_of[4], (EXPERTS * SLICES, HID, D), D ** -0.5, 0.09375, ((0, 512),))
    down_weight = noise(key_of[5], (EXPERTS * SLICES, HID, D), FF ** -0.5, 0.15625, ((0, 512),))
    return {"tokens": tokens, "expert_ids": expert_ids, "gate_ints": gate_ints, "gate_weight": gate_weight, "up_weight": up_weight, "down_weight": down_weight}


def reference(tokens, expert_ids, gate_ints, gate_weight, up_weight, down_weight):
    shares = gate_ints.astype(jnp.float32)
    shares = shares / jnp.sum(shares, axis=1, keepdims=True)
    flat_ids = expert_ids.reshape(-1)
    flat_shares = shares.reshape(-1)
    row_limit = N_DP * MOST
    model_width = tokens.shape[1]
    gate_all = gate_weight.reshape(EXPERTS, FF, model_width)
    up_all = up_weight.reshape(EXPERTS, FF, model_width)
    down_all = down_weight.reshape(EXPERTS, SLICES, HID, model_width)

    def one_expert(expert):
        chosen = flat_ids == expert
        (entries,) = jnp.nonzero(chosen, size=row_limit, fill_value=0)
        entries = entries.astype(jnp.int32)
        is_valid = jnp.arange(row_limit, dtype=jnp.int32) < jnp.sum(chosen.astype(jnp.int32))
        row_ids = entries // TOP
        picked = tokens[row_ids]
        gate_proj = jnp.dot(picked, gate_all[expert].T, preferred_element_type=jnp.float32)
        up_proj = jnp.dot(picked, up_all[expert].T, preferred_element_type=jnp.float32)
        hidden = (jax.nn.silu(gate_proj) * up_proj).astype(jnp.bfloat16).reshape(row_limit, SLICES, HID)
        parts = jnp.einsum("nsh,shd->nsd", hidden.astype(jnp.float32), down_all[expert].astype(jnp.float32))
        parts = parts.astype(jnp.bfloat16)
        result = jnp.sum(parts.astype(jnp.float32), axis=1)
        weight = jnp.where(is_valid, flat_shares[entries], jnp.zeros((), jnp.float32))
        return row_ids, weight[:, None] * result

    row_ids, contrib = lax.map(one_expert, jnp.arange(EXPERTS, dtype=jnp.int32))
    mixed = jnp.zeros((tokens.shape[0], model_width), jnp.float32)
    mixed = mixed.at[row_ids.reshape(-1)].add(contrib.reshape(-1, model_width))
    return mixed.astype(jnp.bfloat16)
```

```python
import functools

import jax
import jax.numpy as jnp
from jax import lax
from jax.experimental import pallas as pl
from jax.experimental.pallas import tpu as pltpu
from jax.sharding import PartitionSpec as P

SLICES = 8
CAP = 10
BF = jnp.bfloat16
F32 = jnp.float32
HIGH = lax.Precision.HIGHEST


def quotient(x, n, top):
    mul = (1 << 16) // n + 1
    assert all((v * mul) >> 16 == v // n for v in range(top))
    return (x * mul) >> 16


def iota(shape, dim):
    return lax.broadcasted_iota(jnp.int32, shape, dim)


def dot32(a, b):
    return jnp.dot(a, b, preferred_element_type=F32)


def dot_rows(a, b):
    return lax.dot_general(a, b, (((1,), (1,)), ((), ())), preferred_element_type=F32)


def kernel(
    sizes, tokens_ref, ids_ref, gates_ref, wg_hbm, wu_hbm, wd_hbm, out_ref,
    wg, wu, wd, stage32, stage, a0r, tabs, blk, gath, pick, sel, xb, acc, hid,
    pcs, pcr, xs, xr, own, zs, zr, rl, rls, mixw, es32, es, er, fin, finr,
    wsem, a0s, a0q, tbs, tbq, a1s, a1q, bzs, bzq, brs, bxs, bxq, bcs, bcq,
    dcs, dcq, dxs, dxq, dzs, dzq, rss, rsq, e1s, e1q, e2s, e2q,
):
    cols, groups, own_rows, width, hidden = sizes
    zn = 2 * groups
    sw = width // SLICES
    hw = sw // 2
    qn = sw // 128
    block = 2 * SLICES * own_rows
    half = SLICES * own_rows
    slots = SLICES * CAP
    lanes = cols * block
    ring8 = zn == 8

    d = lax.axis_index("dp")
    c = lax.axis_index("expert")
    g = lax.div(d, SLICES)
    i = lax.rem(d, SLICES)
    zb = lax.div(i, 4)
    xl = lax.rem(lax.div(i, 2), 2)
    core = lax.rem(i, 2)
    z = 2 * g + zb
    p = xl * 2 + core
    px = (1 - xl) * 2 + core

    def at_cube(j):
        return {"dp": g * SLICES + j, "expert": c}

    def at_column(k):
        return {"dp": d, "expert": k}

    def at_z(k):
        return {"dp": k * 4 + p, "expert": c}

    x_mate = {"dp": z * 4 + px, "expert": c}
    core_mate = {"dp": z * 4 + xl * 2 + (1 - core), "expert": c}
    z_mate_z = 2 * g + (1 - zb)

    def remote(src, dst, ssem, rsem, dev):
        return pltpu.make_async_remote_copy(
            src_ref=src, dst_ref=dst, send_sem=ssem, recv_sem=rsem,
            device_id=dev, device_id_type=pl.DeviceIdType.MESH,
        )

    loads = [
        pltpu.make_async_copy(wg_hbm.at[0], wg, wsem.at[0]),
        pltpu.make_async_copy(wu_hbm.at[0], wu, wsem.at[1]),
        pltpu.make_async_copy(wd_hbm.at[0], wd, wsem.at[2]),
    ]
    for load in loads:
        load.start()

    barrier = pltpu.get_barrier_semaphore()

    def signal(dev):
        pl.semaphore_signal(barrier, inc=1, device_id=dev, device_id_type=pl.DeviceIdType.MESH)

    for k in range(1, SLICES):
        signal(at_cube(lax.rem(i + k, SLICES)))
    for k in range(1, cols):
        signal(at_column(lax.rem(c + k, cols)))
    for k in range(1, groups):
        other = lax.rem(g + k, groups)
        signal(at_z(2 * other))
        signal(at_z(2 * other + 1))

    tok = tokens_ref[...].astype(F32)
    stage32[...] = jnp.zeros_like(stage32)
    for k in range(SLICES * qn):
        stage32[4 * k : 4 * k + own_rows, :] = tok[:, 128 * k : 128 * (k + 1)]
    stage[...] = stage32[...].astype(BF).reshape(stage.shape)

    ids = ids_ref[...]
    gates = gates_ref[...].astype(F32)
    shares = gates / jnp.sum(gates, axis=1, keepdims=True)
    rows = ids.shape[0]
    lane = iota((rows, 128), 1)
    cat = jnp.zeros((rows, 128), F32)
    for k in range(groups):
        hit = ids == c * groups + k
        named = jnp.sum(jnp.where(hit, 1.0, 0.0), axis=1, keepdims=True)
        weight = jnp.sum(jnp.where(hit, shares, 0.0), axis=1, keepdims=True)
        cat = jnp.where(lane == k, named, cat)
        cat = jnp.where(lane == 4 + k, weight, cat)
    lower = jnp.where(iota((rows, rows), 1) < iota((rows, rows), 0), 1.0, 0.0)
    rank = dot32(lower.astype(BF), cat.astype(BF))
    base = (i * CAP + 1).astype(F32)
    table = jnp.where(lane < 4, jnp.where(cat > 0.0, rank + base, 0.0), cat)
    table = jnp.concatenate([table, jnp.zeros((128 - rows, 128), F32)], axis=0)
    tabs[i] = jnp.transpose(table)[0:8, :]
    a0r[i] = stage[i]

    pl.semaphore_wait(barrier, SLICES - 1 + cols - 1 + zn - 2)

    def slice_copy(j):
        return remote(stage.at[j], a0r.at[i], a0s.at[j], a0q.at[i], at_cube(j))

    def table_copy(j):
        return remote(tabs.at[i], tabs.at[i], tbs.at[j], tbq.at[i], at_cube(j))

    for k in range(1, SLICES):
        slice_copy(lax.rem(i + k, SLICES)).start()
    for k in range(1, SLICES):
        table_copy(lax.rem(i + k, SLICES)).start()
    for k in range(1, SLICES):
        j = lax.rem(i + k, SLICES)
        remote(stage.at[j], a0r.at[j], a0s.at[j], a0q.at[j], at_cube(j)).wait_recv()

    flat = a0r[...].reshape(SLICES * 16, 128)
    row = iota((block, SLICES * 16), 0)
    hrow = jnp.where(row >= half, 1, 0)
    rem = row - half * hrow
    dpr = quotient(rem, own_rows, half)
    tgt = dpr * 16 + (2 * hrow) * 4 + (rem - own_rows * dpr)
    colk = iota((block, SLICES * 16), 1)
    for q in range(2):
        perm = jnp.where(colk == tgt + 4 * q, 1.0, 0.0).astype(BF)
        blk[:, 128 * q : 128 * (q + 1)] = dot32(perm, flat).astype(BF)

    def block_copy(k):
        return remote(blk, gath.at[c], a1s.at[k], a1q.at[c], at_column(k))

    def send_block(k, _):
        block_copy(lax.rem(c + k, cols)).start()
        return 0

    lax.fori_loop(1, cols, send_block, 0)
    gath[c] = blk[...]

    for k in range(1, SLICES):
        j = lax.rem(i + k, SLICES)
        remote(tabs.at[j], tabs.at[j], tbs.at[j], tbq.at[j], at_cube(j)).wait_recv()
    flat_tabs = tabs[...].reshape(SLICES * 8, 128)

    lm = iota((128, lanes), 1)
    cm = quotient(lm, block, lanes)
    rm = lm - block * cm
    hm = jnp.where(rm >= half, 1, 0)
    rm = rm - half * hm
    dm = quotient(rm, own_rows, half)
    tm = own_rows * cm + (rm - own_rows * dm)
    spread = jnp.where(iota((128, lanes), 0) == tm, 1.0, 0.0)
    wide = jnp.dot(flat_tabs, spread, precision=HIGH, preferred_element_type=F32)
    wide = jnp.where((iota((SLICES * 8, lanes), 0) >> 3) == dm[0 : SLICES * 8], wide, 0.0)
    wide = jnp.sum(wide.reshape(SLICES, 8, lanes), axis=0)
    slot_id = (iota((slots, lanes), 0) + 1).astype(F32)
    for h in range(2):
        for k in range(groups):
            key = jnp.where(hm[0:1] == h, wide[k : k + 1], 0.0)
            pick[h, k * slots : (k + 1) * slots, :] = jnp.where(
                slot_id == key, 1.0, 0.0
            ).astype(BF)

    mn = cols * half
    rows_m = iota((mn, 128), 0)
    cr = quotient(rows_m, half, mn)
    rr = rows_m - half * cr
    dr = quotient(rr, own_rows, half)
    tr = own_rows * cr + (rr - own_rows * dr)
    spread_t = jnp.where(iota((mn, 128), 1) == tr, 1.0, 0.0)
    tall = jnp.dot(spread_t, jnp.transpose(flat_tabs), precision=HIGH, preferred_element_type=F32)
    lane_t = iota((mn, SLICES * 8), 1)
    tall = jnp.where((lane_t >> 3) == dr[:, 0 : SLICES * 8], tall, 0.0)
    lane_w = iota((mn, zn * slots), 1)
    lz = quotient(lane_w, slots, zn * slots)
    slot_w = (lane_w - slots * lz + 1).astype(F32)
    lg = lz >> 1
    mix = jnp.zeros((mn, zn * slots), F32)
    for k in range(groups):
        key = jnp.sum(jnp.where((lane_t & 7) == k, tall, 0.0), axis=1, keepdims=True)
        wgt = jnp.sum(jnp.where((lane_t & 7) == 4 + k, tall, 0.0), axis=1, keepdims=True)
        mix = jnp.where((lg == k) & (slot_w == key), wgt, mix)
    mixw[...] = mix.astype(BF)

    def wait_block(k, _):
        j = lax.rem(c + k, cols)
        remote(blk, gath.at[j], a1s.at[j], a1q.at[j], at_column(j)).wait_recv()
        return 0

    lax.fori_loop(1, cols, wait_block, 0)

    tokens_all = gath[...].reshape(lanes, hw)
    for h in range(2):
        got = dot32(pick[h], tokens_all).astype(BF)
        sel[:, :, hw * h : hw * (h + 1)] = got.reshape(groups, slots, hw)

    def zmod(k):
        return lax.rem(z + k, zn)

    def out_copy(k):
        return remote(
            sel.at[lax.div(k, 2)], xb.at[p, zb, g], bzs.at[k], bzq.at[z], at_z(k)
        )

    far = [k for k in range(1, zn) if not (ring8 and k == 4)]
    for k in sorted(far, key=lambda k: -min(k, zn - k)):
        out_copy(zmod(k)).start()
    xb[p, zb, g] = sel[g]

    def in_z(k):
        ref = xb.at[p, lax.rem(k, 2), lax.div(k, 2)]
        return remote(ref, ref, bzs.at[k], bzq.at[k], at_z(k))

    def relay_copy(k):
        ref = xb.at[p, lax.rem(k, 2), lax.div(k, 2)]
        return remote(ref, ref, brs.at[0], bzq.at[k], at_z(z_mate_z))

    def x_copy(k, pos):
        ref = xb.at[pos, lax.rem(k, 2), lax.div(k, 2)]
        return remote(ref, ref, bxs.at[k], bxq.at[k], x_mate)

    def c_copy(k, pos, which):
        ref = xb.at[pos, lax.rem(k, 2), lax.div(k, 2)]
        return remote(ref, ref, bcs.at[which * zn + k], bcq.at[which * zn + k], core_mate)

    if ring8:
        kr = 5 - 2 * zb
        order = [0, 1, 7, kr, 2, 6, 8 - kr, 4]
    else:
        order = list(range(zn))
    for n, k in enumerate(order):
        src = zmod(k)
        if n > 0:
            in_z(src).wait_recv()
        if ring8 and n == 3:
            relay_copy(src).start()
        x_copy(src, p).start()
        c_copy(src, p, 0).start()

    loads[0].wait()
    loads[1].wait()

    def project(pos, first):
        for b in range(2):
            off = pl.multiple_of((b * 4 + pos) * sw, sw)
            part = xb[pos, b].reshape(groups * slots, sw)
            up = dot_rows(part, wu[:, pl.ds(off, sw)])
            gate = dot_rows(part, wg[:, pl.ds(off, sw)])
            if first and b == 0:
                acc[0] = gate
                acc[1] = up
            else:
                acc[0] += gate
                acc[1] += up

    project(p, True)
    for k in order:
        src = zmod(k)
        x_copy(src, px).wait_recv()
        c_copy(src, px, 1).start()
    project(px, False)
    pc = xl * 2 + (1 - core)
    pxc = (1 - xl) * 2 + (1 - core)
    for k in order:
        c_copy(zmod(k), pc, 0).wait_recv()
    project(pc, False)
    for k in order:
        c_copy(zmod(k), pxc, 1).wait_recv()
    project(pxc, False)

    gate = acc[0]
    hid[...] = (gate / (1.0 + jnp.exp(-gate)) * acc[1]).astype(BF)
    loads[2].wait()

    def down(b, pos):
        off = pl.multiple_of((b * 4 + pos) * sw, sw)
        return dot32(hid[...], wd[:, pl.ds(off, sw)]).reshape(groups, slots, sw)

    def pc_copy(which, b):
        return remote(
            pcs.at[which, b], pcr.at[which, b],
            dcs.at[2 * which + b], dcq.at[2 * which + b], core_mate,
        )

    def xd_copy(k):
        b, e = lax.rem(k, 2), lax.div(k, 2)
        return remote(xs.at[b, e], xr.at[b, e], dxs.at[k], dxq.at[k], x_mate)

    if ring8:
        back = [4, 8 - kr, kr, 2, 6, 1, 7, 0]
    else:
        back = list(range(zn - 1, -1, -1))
    for b in range(2):
        pcs[0, b] = down(b, pxc).astype(BF)
        pc_copy(0, b).start()
    for b in range(2):
        mine = down(b, px)
        pc_copy(0, b).wait_recv()
        xs[b] = (mine + pcr[0, b].astype(F32)).astype(BF)
    for k in back:
        xd_copy(zmod(k)).start()
    for b in range(2):
        pcs[1, b] = down(b, pc).astype(BF)
        pc_copy(1, b).start()
    for b in range(2):
        mine = down(b, p)
        pc_copy(1, b).wait_recv()
        own[b] = mine + pcr[1, b].astype(F32)

    def home_copy(k):
        return remote(zs.at[k], zr.at[z], dzs.at[k], dzq.at[z], at_z(k))

    def lent_copy():
        return remote(rls, rl, rss.at[0], rsq.at[0], at_z(z_mate_z))

    for n, k in enumerate(back):
        dst = zmod(k)
        b, e = lax.rem(dst, 2), lax.div(dst, 2)
        xd_copy(dst).wait_recv()
        total = own[b, e] + xr[b, e].astype(F32)
        if n == len(back) - 1:
            zr[z] = total.astype(BF)
        elif ring8 and n == 0:
            rls[...] = total.astype(BF)
            lent_copy().start()
        else:
            if ring8 and n == 2:
                lent_copy().wait_recv()
                total = total + rl[...].astype(F32)
            zs[dst] = total.astype(BF)
            home_copy(dst).start()
    if ring8:
        zr[zmod(4)] = jnp.zeros((slots, sw), BF)
    for n, k in enumerate(back[:-1]):
        if ring8 and n == 0:
            continue
        src = zmod(zn - k)
        remote(zs.at[src], zr.at[src], dzs.at[src], dzq.at[src], at_z(src)).wait_recv()

    for h in range(2):
        part = zr[:, :, hw * h : hw * (h + 1)].reshape(zn * slots, hw)
        es32[:, half * h : half * (h + 1), :] = dot32(mixw[...], part).reshape(cols, half, hw)
    es[...] = es32[...].astype(BF)

    def sum_copy(k):
        return remote(es.at[k], er.at[c], e1s.at[k], e1q.at[c], at_column(k))

    def send_sum(k, _):
        sum_copy(lax.rem(c + k, cols)).start()
        return 0

    lax.fori_loop(1, cols, send_sum, 0)
    er[c] = es[c]

    def wait_sum(k, _):
        j = lax.rem(c + k, cols)
        remote(es.at[j], er.at[j], e1s.at[j], e1q.at[j], at_column(j)).wait_recv()
        return 0

    lax.fori_loop(1, cols, wait_sum, 0)
    total = er[0].astype(F32)
    for k in range(1, cols):
        total = total + er[k].astype(F32)
    total = total.astype(BF)

    colb = iota((SLICES * 16, block), 1)
    hcol = jnp.where(colb >= half, 1, 0)
    rem = colb - half * hcol
    dpc = quotient(rem, own_rows, half)
    tgt = dpc * 16 + (2 * hcol) * 4 + (rem - own_rows * dpc)
    rowk = iota((SLICES * 16, block), 0)
    tiles = jnp.zeros((SLICES * 16, 128), F32)
    for q in range(2):
        perm = jnp.where(rowk == tgt + 4 * q, 1.0, 0.0).astype(BF)
        tiles = tiles + dot32(perm, total[:, 128 * q : 128 * (q + 1)])
    fin[...] = tiles.astype(BF).reshape(fin.shape)
    finr[i] = fin[i]

    for k in range(1, SLICES):
        j = lax.rem(i + k, SLICES)
        remote(fin.at[j], finr.at[i], e2s.at[j], e2q.at[i], at_cube(j)).start()
    for k in range(1, SLICES):
        j = lax.rem(i + k, SLICES)
        remote(fin.at[j], finr.at[j], e2s.at[j], e2q.at[j], at_cube(j)).wait_recv()
    stage32[...] = finr[...].astype(F32).reshape(SLICES * 16, 128)
    out_ref[...] = jnp.concatenate(
        [stage32[4 * k : 4 * k + own_rows, :] for k in range(SLICES * qn)], axis=1
    ).astype(BF)

    for k in range(1, SLICES):
        j = lax.rem(i + k, SLICES)
        slice_copy(j).wait_send()
        table_copy(j).wait_send()
        remote(fin.at[j], finr.at[i], e2s.at[j], e2q.at[i], at_cube(j)).wait_send()

    def wait_columns(k, _):
        j = lax.rem(c + k, cols)
        block_copy(j).wait_send()
        sum_copy(j).wait_send()
        return 0

    lax.fori_loop(1, cols, wait_columns, 0)
    for k in far:
        out_copy(zmod(k)).wait_send()
        home_copy(zmod(k)).wait_send()
    if ring8:
        relay_copy(zmod(kr)).wait_send()
        lent_copy().wait_send()
    for k in range(zn):
        x_copy(k, p).wait_send()
        c_copy(k, p, 0).wait_send()
        c_copy(k, px, 1).wait_send()
        xd_copy(k).wait_send()
    for which in range(2):
        for b in range(2):
            pc_copy(which, b).wait_send()


def local(tokens, expert_ids, gate_ints, gate_weight, up_weight, down_weight):
    groups = lax.axis_size("dp") // SLICES
    cols = lax.axis_size("expert")
    own_rows, width = tokens.shape
    hidden = gate_weight.shape[1]
    zn = 2 * groups
    sw = width // SLICES
    hw = sw // 2
    block = 2 * SLICES * own_rows
    half = SLICES * own_rows
    slots = SLICES * CAP
    vmem = pltpu.VMEM
    dma = pltpu.SemaphoreType.DMA
    sizes = (cols, groups, own_rows, width, hidden)
    scratch = [
        vmem((hidden, width), BF),
        vmem((hidden, width), BF),
        vmem((hidden, width), BF),
        vmem((SLICES * 16, 128), F32),
        vmem((SLICES, 16, 128), BF),
        vmem((SLICES, 16, 128), BF),
        vmem((SLICES, 8, 128), F32),
        vmem((block, hw), BF),
        vmem((cols, block, hw), BF),
        vmem((2, groups * slots, cols * block), BF),
        vmem((groups, slots, sw), BF),
        vmem((4, 2, groups, slots, sw), BF),
        vmem((2, groups * slots, hidden), F32),
        vmem((groups * slots, hidden), BF),
        vmem((2, 2, groups, slots, sw), BF),
        vmem((2, 2, groups, slots, sw), BF),
        vmem((2, groups, slots, sw), BF),
        vmem((2, groups, slots, sw), BF),
        vmem((2, groups, slots, sw), F32),
        vmem((zn, slots, sw), BF),
        vmem((zn, slots, sw), BF),
        vmem((slots, sw), BF),
        vmem((slots, sw), BF),
        vmem((cols * half, zn * slots), BF),
        vmem((cols, block, hw), F32),
        vmem((cols, block, hw), BF),
        vmem((cols, block, hw), BF),
        vmem((SLICES, 16, 128), BF),
        vmem((SLICES, 16, 128), BF),
        dma((3,)),
        dma((SLICES,)), dma((SLICES,)), dma((SLICES,)), dma((SLICES,)),
        dma((cols,)), dma((cols,)),
        dma((zn,)), dma((zn,)), dma((1,)),
        dma((zn,)), dma((zn,)), dma((2 * zn,)), dma((2 * zn,)),
        dma((4,)), dma((4,)), dma((zn,)), dma((zn,)),
        dma((zn,)), dma((zn,)), dma((1,)), dma((1,)),
        dma((cols,)), dma((cols,)), dma((SLICES,)), dma((SLICES,)),
    ]
    return pl.pallas_call(
        functools.partial(kernel, sizes),
        out_shape=jax.ShapeDtypeStruct((own_rows, width), BF),
        in_specs=[pl.BlockSpec(memory_space=pltpu.VMEM)] * 3
        + [pl.BlockSpec(memory_space=pl.ANY)] * 3,
        out_specs=pl.BlockSpec(memory_space=pltpu.VMEM),
        scratch_shapes=scratch,
        compiler_params=pltpu.CompilerParams(
            collective_id=0, has_side_effects=True, vmem_limit_bytes=56 * 1024 * 1024
        ),
    )(tokens, expert_ids, gate_ints, gate_weight, up_weight, down_weight)


def solution(mesh):
    return jax.shard_map(
        local,
        mesh=mesh,
        in_specs=(
            P(("dp", "expert"), None),
            P("dp", None),
            P("dp", None),
            P(("expert", "dp"), None, None),
            P(("expert", "dp"), None, None),
            P(("expert", "dp"), None, None),
        ),
        out_specs=P(("dp", "expert"), None),
        check_vma=False,
    )
```

```python
import functools

import jax
import jax.numpy as jnp
from jax import lax
from jax.experimental import pallas as pl
from jax.experimental.pallas import tpu as pltpu
from jax.sharding import PartitionSpec as P

SLICES = 8
CAP = 10
EARLY = 3
LATE = 6
BF = jnp.bfloat16
F32 = jnp.float32
HIGH = lax.Precision.HIGHEST


def quotient(x, n, top):
    mul = (1 << 16) // n + 1
    assert all((v * mul) >> 16 == v // n for v in range(top))
    return (x * mul) >> 16


def iota(shape, dim):
    return lax.broadcasted_iota(jnp.int32, shape, dim)


def dot32(a, b):
    return jnp.dot(a, b, preferred_element_type=F32)


def dot_rows(a, b):
    return lax.dot_general(a, b, (((1,), (1,)), ((), ())), preferred_element_type=F32)


def kernel(
    sizes, tokens_ref, ids_ref, gates_ref, wg_hbm, wu_hbm, wd_hbm, out_ref,
    wg, wu, wd, stage32, stage, a0r, tabs, blk, gath, pick, sel, xb, acc, hid,
    pcs, pcr, xs, xr, own, zs, zr, rl, rls, mixw, es32, es, er, fin, finr,
    wsem, a0s, a0q, tbs, tbq, a1s, a1q, bzs, bzq, brs, bxs, bxq, bcs, bcq,
    dcs, dcq, dxs, dxq, dzs, dzq, rss, rsq, e1s, e1q, e2s, e2q,
):
    cols, groups, own_rows, width, hidden = sizes
    zn = 2 * groups
    sw = width // SLICES
    hw = sw // 2
    qn = sw // 128
    block = 2 * SLICES * own_rows
    half = SLICES * own_rows
    slots = SLICES * CAP
    lanes = cols * block
    ring8 = zn == 8

    d = lax.axis_index("dp")
    c = lax.axis_index("expert")
    g = lax.div(d, SLICES)
    i = lax.rem(d, SLICES)
    zb = lax.div(i, 4)
    xl = lax.rem(lax.div(i, 2), 2)
    core = lax.rem(i, 2)
    z = 2 * g + zb
    p = xl * 2 + core
    px = (1 - xl) * 2 + core

    def at_cube(j):
        return {"dp": g * SLICES + j, "expert": c}

    def at_column(k):
        return {"dp": d, "expert": k}

    def at_z(k):
        return {"dp": k * 4 + p, "expert": c}

    x_mate = {"dp": z * 4 + px, "expert": c}
    core_mate = {"dp": z * 4 + xl * 2 + (1 - core), "expert": c}
    z_mate_z = 2 * g + (1 - zb)

    def remote(src, dst, ssem, rsem, dev):
        return pltpu.make_async_remote_copy(
            src_ref=src, dst_ref=dst, send_sem=ssem, recv_sem=rsem,
            device_id=dev, device_id_type=pl.DeviceIdType.MESH,
        )

    sent = []

    def start(copy):
        copy.start()
        sent.append(copy)

    def finish():
        for copy in sent:
            copy.wait_send()

    loads = [
        pltpu.make_async_copy(wg_hbm.at[0], wg, wsem.at[0]),
        pltpu.make_async_copy(wu_hbm.at[0], wu, wsem.at[1]),
        pltpu.make_async_copy(wd_hbm.at[0], wd, wsem.at[2]),
    ]
    for load in loads:
        load.start()

    barrier = pltpu.get_barrier_semaphore()

    def signal(dev):
        pl.semaphore_signal(barrier, inc=1, device_id=dev, device_id_type=pl.DeviceIdType.MESH)

    for k in range(1, SLICES):
        signal(at_cube(lax.rem(i + k, SLICES)))
    for k in range(1, cols):
        signal(at_column(lax.rem(c + k, cols)))
    for k in range(1, groups):
        other = lax.rem(g + k, groups)
        signal(at_z(2 * other))
        signal(at_z(2 * other + 1))

    tok = tokens_ref[...].astype(F32)
    stage32[...] = jnp.zeros_like(stage32)
    for k in range(SLICES * qn):
        stage32[4 * k : 4 * k + own_rows, :] = tok[:, 128 * k : 128 * (k + 1)]
    stage[...] = stage32[...].astype(BF).reshape(stage.shape)

    ids = ids_ref[...]
    gates = gates_ref[...].astype(F32)
    shares = gates / jnp.sum(gates, axis=0, keepdims=True)
    rows = ids.shape[1]
    line = iota((8, rows), 0)
    cat = jnp.zeros((8, rows), F32)
    for k in range(groups):
        hit = ids == c * groups + k
        named = jnp.sum(jnp.where(hit, 1.0, 0.0), axis=0, keepdims=True)
        weight = jnp.sum(jnp.where(hit, shares, 0.0), axis=0, keepdims=True)
        cat = jnp.where(line == k, named, cat)
        cat = jnp.where(line == 4 + k, weight, cat)
    upper = jnp.where(iota((rows, rows), 0) < iota((rows, rows), 1), 1.0, 0.0)
    rank = dot32(cat.astype(BF), upper.astype(BF))
    base = (i * CAP + 1).astype(F32)
    table = jnp.where(line < 4, jnp.where(cat > 0.0, rank + base, 0.0), cat)
    tabs[i] = jnp.concatenate([table, jnp.zeros((8, 128 - rows), F32)], axis=1)
    a0r[i] = stage[i]

    pl.semaphore_wait(barrier, SLICES - 1 + cols - 1 + zn - 2)

    def slice_copy(j):
        return remote(stage.at[j], a0r.at[i], a0s.at[j], a0q.at[i], at_cube(j))

    def table_copy(j):
        return remote(tabs.at[i], tabs.at[i], tbs.at[j], tbq.at[i], at_cube(j))

    for k in range(1, SLICES):
        start(slice_copy(lax.rem(i + k, SLICES)))
    for k in range(1, SLICES):
        start(table_copy(lax.rem(i + k, SLICES)))
    for k in range(1, SLICES):
        j = lax.rem(i + k, SLICES)
        remote(stage.at[j], a0r.at[j], a0s.at[j], a0q.at[j], at_cube(j)).wait_recv()

    flat = a0r[...].reshape(SLICES * 16, 128)
    row = iota((block, SLICES * 16), 0)
    hrow = jnp.where(row >= half, 1, 0)
    rem = row - half * hrow
    dpr = quotient(rem, own_rows, half)
    tgt = dpr * 16 + hrow * 4 + (rem - own_rows * dpr)
    colk = iota((block, SLICES * 16), 1)

    def block_copy(k, t):
        return remote(blk.at[t], gath.at[t, c], a1s.at[t, k], a1q.at[t, c], at_column(k))

    for t in range(2):
        perm = jnp.where(colk == tgt + 8 * t, 1.0, 0.0).astype(BF)
        blk[t] = dot32(perm, flat).astype(BF)
        for k in range(1, cols):
            start(block_copy(lax.rem(c + k, cols), t))
        gath[t, c] = blk[t]

    for k in range(1, SLICES):
        j = lax.rem(i + k, SLICES)
        remote(tabs.at[j], tabs.at[j], tbs.at[j], tbq.at[j], at_cube(j)).wait_recv()
    flat_tabs = tabs[...].reshape(SLICES * 8, 128)

    lm = iota((128, lanes), 1)
    cm = quotient(lm, block, lanes)
    rm = lm - block * cm
    hm = jnp.where(rm >= half, 1, 0)
    rm = rm - half * hm
    dm = quotient(rm, own_rows, half)
    tm = own_rows * cm + (rm - own_rows * dm)
    spread = jnp.where(iota((128, lanes), 0) == tm, 1.0, 0.0)
    wide = jnp.dot(flat_tabs, spread, precision=HIGH, preferred_element_type=F32)
    wide = jnp.where((iota((SLICES * 8, lanes), 0) >> 3) == dm[0 : SLICES * 8], wide, 0.0)
    wide = jnp.sum(wide.reshape(SLICES, 8, lanes), axis=0)
    slot_id = (iota((slots, lanes), 0) + 1).astype(F32)
    for h in range(2):
        for k in range(groups):
            key = jnp.where(hm[0:1] == h, wide[k : k + 1], 0.0)
            pick[h, k * slots : (k + 1) * slots, :] = jnp.where(
                slot_id == key, 1.0, 0.0
            ).astype(BF)

    def make_mix():
        mn = cols * half
        rows_m = iota((mn, 128), 0)
        cr = quotient(rows_m, half, mn)
        rr = rows_m - half * cr
        dr = quotient(rr, own_rows, half)
        tr = own_rows * cr + (rr - own_rows * dr)
        spread_t = jnp.where(iota((mn, 128), 1) == tr, 1.0, 0.0)
        tall = jnp.dot(spread_t, jnp.transpose(flat_tabs), precision=HIGH, preferred_element_type=F32)
        lane_t = iota((mn, SLICES * 8), 1)
        tall = jnp.where((lane_t >> 3) == dr[:, 0 : SLICES * 8], tall, 0.0)
        lane_w = iota((mn, zn * slots), 1)
        lz = quotient(lane_w, slots, zn * slots)
        slot_w = (lane_w - slots * lz + 1).astype(F32)
        lg = lz >> 1
        mix = jnp.zeros((mn, zn * slots), F32)
        for k in range(groups):
            key = jnp.sum(jnp.where((lane_t & 7) == k, tall, 0.0), axis=1, keepdims=True)
            wgt = jnp.sum(jnp.where((lane_t & 7) == 4 + k, tall, 0.0), axis=1, keepdims=True)
            mix = jnp.where((lg == k) & (slot_w == key), wgt, mix)
        mixw[...] = mix.astype(BF)

    def zmod(k):
        return lax.rem(z + k, zn)

    def out_copy(k, t):
        return remote(
            sel.at[t, lax.div(k, 2)], xb.at[t, p, zb, g], bzs.at[t, k], bzq.at[t, z], at_z(k)
        )

    def spot(k, pos, t):
        return xb.at[t, pos, lax.rem(k, 2), lax.div(k, 2)]

    def in_z(k, t):
        ref = spot(k, p, t)
        return remote(ref, ref, bzs.at[t, k], bzq.at[t, k], at_z(k))

    def relay_copy(k, t):
        ref = spot(k, p, t)
        return remote(ref, ref, brs.at[t], bzq.at[t, k], at_z(z_mate_z))

    def x_copy(k, pos, t):
        ref = spot(k, pos, t)
        return remote(ref, ref, bxs.at[t, k], bxq.at[t, k], x_mate)

    def c_copy(k, pos, which, t):
        ref = spot(k, pos, t)
        return remote(ref, ref, bcs.at[t, which * zn + k], bcq.at[t, which * zn + k], core_mate)

    if ring8:
        kr = 5 - 2 * zb
        order = [0, 1, 7, kr, 2, 6, 8 - kr, 4]
        leave = order[1:7]
    else:
        order = list(range(zn))
        leave = order[1:]

    def pass_on(k, t):
        start(x_copy(k, p, t))
        start(c_copy(k, p, 0, t))

    def dispatch(t):
        def wait_block(k, _):
            j = lax.rem(c + k, cols)
            remote(
                blk.at[t], gath.at[t, j], a1s.at[t, j], a1q.at[t, j], at_column(j)
            ).wait_recv()
            return 0

        lax.fori_loop(1, cols, wait_block, 0)
        tokens_all = gath[t].reshape(lanes, 128)
        for h in range(2):
            got = dot32(pick[h], tokens_all).astype(BF)
            sel[t, :, :, 128 * h : 128 * (h + 1)] = got.reshape(groups, slots, 128)
        for k in leave:
            start(out_copy(zmod(k), t))
        xb[t, p, zb, g] = sel[t, g]
        pass_on(z, t)

    def arrive(n, t):
        src = zmod(order[n])
        in_z(src, t).wait_recv()
        if ring8 and n == 3:
            start(relay_copy(src, t))
        pass_on(src, t)

    early = EARLY if ring8 else 1
    dispatch(0)
    for n in range(1, early):
        arrive(n, 0)
    dispatch(1)
    for n in range(early, zn):
        arrive(n, 0)

    loads[0].wait()
    loads[1].wait()

    def project(pos, t, first=False):
        for b in range(2):
            off = pl.multiple_of((b * 4 + pos) * sw + t * hw, hw)
            part = xb[t, pos, b].reshape(groups * slots, hw)
            up = dot_rows(part, wu[:, pl.ds(off, hw)])
            gate = dot_rows(part, wg[:, pl.ds(off, hw)])
            if first and b == 0:
                acc[0] = gate
                acc[1] = up
            else:
                acc[0] += gate
                acc[1] += up

    pc = xl * 2 + (1 - core)
    pxc = (1 - xl) * 2 + (1 - core)

    def cross(n, t):
        src = zmod(order[n])
        x_copy(src, px, t).wait_recv()
        start(c_copy(src, px, 1, t))

    def wait_core(pos, which, t):
        for k in range(zn):
            c_copy(k, pos, which, t).wait_recv()

    for n in range(1, zn):
        arrive(n, 1)
    for n in range(zn):
        cross(n, 0)
    project(p, 0, True)
    project(p, 1)
    for n in range(zn // 2):
        cross(n, 1)
    project(px, 0)
    wait_core(pc, 0, 0)
    project(pc, 0)
    make_mix()
    for n in range(zn // 2, zn):
        cross(n, 1)
    wait_core(pxc, 1, 0)
    project(pxc, 0)
    project(px, 1)
    wait_core(pc, 0, 1)
    project(pc, 1)
    wait_core(pxc, 1, 1)
    project(pxc, 1)

    gate = acc[0]
    hid[...] = (gate / (1.0 + jnp.exp(-gate)) * acc[1]).astype(BF)
    loads[2].wait()

    def down(b, pos, t):
        off = pl.multiple_of((b * 4 + pos) * sw + t * hw, hw)
        return dot32(hid[...], wd[:, pl.ds(off, hw)]).reshape(groups, slots, hw)

    def pc_copy(which, b, t):
        n = 4 * which + 2 * t + b
        return remote(pcs.at[which, t, b], pcr.at[which, t, b], dcs.at[n], dcq.at[n], core_mate)

    def xd_copy(k, t):
        b, e = lax.rem(k, 2), lax.div(k, 2)
        return remote(xs.at[t, b, e], xr.at[t, b, e], dxs.at[t, k], dxq.at[t, k], x_mate)

    if ring8:
        back = [4, 8 - kr, kr, 2, 6, 1, 7, 0]
    else:
        back = list(range(zn - 1, -1, -1))
    for t in range(2):
        for b in range(2):
            pcs[0, t, b] = down(b, pxc, t).astype(BF)
            start(pc_copy(0, b, t))
    for t in range(2):
        for b in range(2):
            mine = down(b, px, t)
            pc_copy(0, b, t).wait_recv()
            xs[t, b] = (mine + pcr[0, t, b].astype(F32)).astype(BF)
        for k in back:
            start(xd_copy(zmod(k), t))
    for t in range(2):
        for b in range(2):
            pcs[1, t, b] = down(b, pc, t).astype(BF)
            start(pc_copy(1, b, t))
    for t in range(2):
        for b in range(2):
            mine = down(b, p, t)
            pc_copy(1, b, t).wait_recv()
            own[t, b] = mine + pcr[1, t, b].astype(F32)

    def home_copy(k, t):
        return remote(zs.at[t, k], zr.at[t, z], dzs.at[t, k], dzq.at[t, z], at_z(k))

    def lent_copy(t):
        return remote(rls.at[t], rl.at[t], rss.at[t], rsq.at[t], at_z(z_mate_z))

    def give_back(n, t):
        dst = zmod(back[n])
        b, e = lax.rem(dst, 2), lax.div(dst, 2)
        xd_copy(dst, t).wait_recv()
        total = own[t, b, e] + xr[t, b, e].astype(F32)
        if n == zn - 1:
            zr[t, z] = total.astype(BF)
        elif ring8 and n == 0:
            rls[t] = total.astype(BF)
            start(lent_copy(t))
        else:
            if ring8 and n == 2:
                lent_copy(t).wait_recv()
                total = total + rl[t].astype(F32)
            zs[t, dst] = total.astype(BF)
            start(home_copy(dst, t))

    def sum_copy(k, t):
        return remote(es.at[t, k], er.at[t, c], e1s.at[t, k], e1q.at[t, c], at_column(k))

    def settle(t):
        if ring8:
            zr[t, zmod(4)] = jnp.zeros((slots, hw), BF)
        for n, k in enumerate(back[:-1]):
            if ring8 and n == 0:
                continue
            src = zmod(zn - k)
            remote(
                zs.at[t, src], zr.at[t, src], dzs.at[t, src], dzq.at[t, src], at_z(src)
            ).wait_recv()
        mixed = dot32(mixw[...], zr[t].reshape(zn * slots, hw))
        for h in range(2):
            es32[:, half * h : half * (h + 1), :] = mixed[:, 128 * h : 128 * (h + 1)].reshape(
                cols, half, 128
            )
        es[t] = es32[...].astype(BF)
        for k in range(1, cols):
            start(sum_copy(lax.rem(c + k, cols), t))
        er[t, c] = es[t, c]

    for n in range(zn):
        give_back(n, 0)
    late = LATE if ring8 else zn - 1
    for n in range(late):
        give_back(n, 1)
    settle(0)
    for n in range(late, zn):
        give_back(n, 1)
    settle(1)

    def column_sum(t):
        def wait_sum(k, _):
            j = lax.rem(c + k, cols)
            remote(
                es.at[t, j], er.at[t, j], e1s.at[t, j], e1q.at[t, j], at_column(j)
            ).wait_recv()
            return 0

        lax.fori_loop(1, cols, wait_sum, 0)
        total = er[t, 0].astype(F32)
        for k in range(1, cols):
            total = total + er[t, k].astype(F32)
        return total.astype(BF)

    colb = iota((SLICES * 16, block), 1)
    hcol = jnp.where(colb >= half, 1, 0)
    rem = colb - half * hcol
    dpc = quotient(rem, own_rows, half)
    tgt = dpc * 16 + hcol * 4 + (rem - own_rows * dpc)
    rowk = iota((SLICES * 16, block), 0)
    tiles = jnp.zeros((SLICES * 16, 128), F32)
    for t in range(2):
        perm = jnp.where(rowk == tgt + 8 * t, 1.0, 0.0).astype(BF)
        tiles = tiles + dot32(perm, column_sum(t))
    fin[...] = tiles.astype(BF).reshape(fin.shape)
    finr[i] = fin[i]

    for k in range(1, SLICES):
        j = lax.rem(i + k, SLICES)
        start(remote(fin.at[j], finr.at[i], e2s.at[j], e2q.at[i], at_cube(j)))
    for k in range(1, SLICES):
        j = lax.rem(i + k, SLICES)
        remote(fin.at[j], finr.at[j], e2s.at[j], e2q.at[j], at_cube(j)).wait_recv()
    stage32[...] = finr[...].astype(F32).reshape(SLICES * 16, 128)
    out_ref[...] = jnp.concatenate(
        [stage32[4 * k : 4 * k + own_rows, :] for k in range(SLICES * qn)], axis=1
    ).astype(BF)

    finish()


def local(tokens, expert_ids, gate_ints, gate_weight, up_weight, down_weight):
    groups = lax.axis_size("dp") // SLICES
    cols = lax.axis_size("expert")
    own_rows, width = tokens.shape
    hidden = gate_weight.shape[1]
    zn = 2 * groups
    sw = width // SLICES
    hw = sw // 2
    block = 2 * SLICES * own_rows
    half = SLICES * own_rows
    slots = SLICES * CAP
    vmem = pltpu.VMEM
    dma = pltpu.SemaphoreType.DMA
    sizes = (cols, groups, own_rows, width, hidden)
    scratch = [
        vmem((hidden, width), BF),
        vmem((hidden, width), BF),
        vmem((hidden, width), BF),
        vmem((SLICES * 16, 128), F32),
        vmem((SLICES, 16, 128), BF),
        vmem((SLICES, 16, 128), BF),
        vmem((SLICES, 8, 128), F32),
        vmem((2, block, 128), BF),
        vmem((2, cols, block, 128), BF),
        vmem((2, groups * slots, cols * block), BF),
        vmem((2, groups, slots, hw), BF),
        vmem((2, 4, 2, groups, slots, hw), BF),
        vmem((2, groups * slots, hidden), F32),
        vmem((groups * slots, hidden), BF),
        vmem((2, 2, 2, groups, slots, hw), BF),
        vmem((2, 2, 2, groups, slots, hw), BF),
        vmem((2, 2, groups, slots, hw), BF),
        vmem((2, 2, groups, slots, hw), BF),
        vmem((2, 2, groups, slots, hw), F32),
        vmem((2, zn, slots, hw), BF),
        vmem((2, zn, slots, hw), BF),
        vmem((2, slots, hw), BF),
        vmem((2, slots, hw), BF),
        vmem((cols * half, zn * slots), BF),
        vmem((cols, block, 128), F32),
        vmem((2, cols, block, 128), BF),
        vmem((2, cols, block, 128), BF),
        vmem((SLICES, 16, 128), BF),
        vmem((SLICES, 16, 128), BF),
        dma((3,)),
        dma((SLICES,)), dma((SLICES,)), dma((SLICES,)), dma((SLICES,)),
        dma((2, cols)), dma((2, cols)),
        dma((2, zn)), dma((2, zn)), dma((2,)),
        dma((2, zn)), dma((2, zn)), dma((2, 2 * zn)), dma((2, 2 * zn)),
        dma((8,)), dma((8,)), dma((2, zn)), dma((2, zn)),
        dma((2, zn)), dma((2, zn)), dma((2,)), dma((2,)),
        dma((2, cols)), dma((2, cols)), dma((SLICES,)), dma((SLICES,)),
    ]
    return pl.pallas_call(
        functools.partial(kernel, sizes),
        out_shape=jax.ShapeDtypeStruct((own_rows, width), BF),
        in_specs=[pl.BlockSpec(memory_space=pltpu.VMEM)] * 3
        + [pl.BlockSpec(memory_space=pl.ANY)] * 3,
        out_specs=pl.BlockSpec(memory_space=pltpu.VMEM),
        scratch_shapes=scratch,
        compiler_params=pltpu.CompilerParams(
            collective_id=0, has_side_effects=True, vmem_limit_bytes=56 * 1024 * 1024
        ),
    )(tokens, expert_ids.T, gate_ints.T, gate_weight, up_weight, down_weight)


def solution(mesh):
    return jax.shard_map(
        local,
        mesh=mesh,
        in_specs=(
            P(("dp", "expert"), None),
            P("dp", None),
            P("dp", None),
            P(("expert", "dp"), None, None),
            P(("expert", "dp"), None, None),
            P(("expert", "dp"), None, None),
        ),
        out_specs=P(("dp", "expert"), None),
        check_vma=False,
    )
```

```python
import functools

import jax
import jax.numpy as jnp
from jax import lax
from jax.experimental import pallas as pl
from jax.experimental.pallas import tpu as pltpu
from jax.sharding import PartitionSpec as P

SLICES = 8
CAP = 10
EARLY = 3
LATE = 6
BF = jnp.bfloat16
F32 = jnp.float32
HIGH = lax.Precision.HIGHEST


def quotient(x, n, top):
    mul = (1 << 16) // n + 1
    assert all((v * mul) >> 16 == v // n for v in range(top))
    return (x * mul) >> 16


def iota(shape, dim):
    return lax.broadcasted_iota(jnp.int32, shape, dim)


def dot32(a, b):
    return jnp.dot(a, b, preferred_element_type=F32)


def dot_rows(a, b):
    return lax.dot_general(a, b, (((1,), (1,)), ((), ())), preferred_element_type=F32)


def kernel(
    sizes, tokens_ref, ids_ref, gates_ref, wg_hbm, wu_hbm, wd_hbm, out_ref,
    wg, wu, wd, stage32, stage, a0r, tabs, blk, gath, pick, sel, xb, acc, hid,
    pcs, pcr, xs, xr, own, zs, zr, rl, rls, mixw, es32, es, er, fin, finr,
    wsem, a0s, a0q, tbs, tbq, a1s, a1q, bzs, bzq, brs, bxs, bxq, bcs, bcq,
    dcs, dcq, dxs, dxq, dzs, dzq, rss, rsq, e1s, e1q, e2s, e2q,
):
    cols, groups, own_rows, width, hidden = sizes
    zn = 2 * groups
    sw = width // SLICES
    hw = sw // 2
    qn = sw // 128
    block = 2 * SLICES * own_rows
    half = SLICES * own_rows
    slots = SLICES * CAP
    lanes = cols * block
    ring8 = zn == 8

    d = lax.axis_index("dp")
    c = lax.axis_index("expert")
    g = lax.div(d, SLICES)
    i = lax.rem(d, SLICES)
    zb = lax.div(i, 4)
    xl = lax.rem(lax.div(i, 2), 2)
    core = lax.rem(i, 2)
    z = 2 * g + zb
    p = xl * 2 + core
    px = (1 - xl) * 2 + core

    def at_cube(j):
        return {"dp": g * SLICES + j, "expert": c}

    def at_column(k):
        return {"dp": d, "expert": k}

    def at_z(k):
        return {"dp": k * 4 + p, "expert": c}

    x_mate = {"dp": z * 4 + px, "expert": c}
    core_mate = {"dp": z * 4 + xl * 2 + (1 - core), "expert": c}
    z_mate_z = 2 * g + (1 - zb)

    def remote(src, dst, ssem, rsem, dev):
        return pltpu.make_async_remote_copy(
            src_ref=src, dst_ref=dst, send_sem=ssem, recv_sem=rsem,
            device_id=dev, device_id_type=pl.DeviceIdType.MESH,
        )

    sent = []

    def start(copy):
        copy.start()
        sent.append(copy)

    def finish(keep=0):
        done = len(sent) - keep
        for copy in sent[:done]:
            copy.wait_send()
        del sent[:done]

    loads = [
        pltpu.make_async_copy(wg_hbm.at[0], wg, wsem.at[0]),
        pltpu.make_async_copy(wu_hbm.at[0], wu, wsem.at[1]),
        pltpu.make_async_copy(wd_hbm.at[0], wd, wsem.at[2]),
    ]
    for load in loads:
        load.start()

    barrier = pltpu.get_barrier_semaphore()

    def signal(dev):
        pl.semaphore_signal(barrier, inc=1, device_id=dev, device_id_type=pl.DeviceIdType.MESH)

    for k in range(1, SLICES):
        signal(at_cube(lax.rem(i + k, SLICES)))
    for k in range(1, cols):
        signal(at_column(lax.rem(c + k, cols)))
    for k in range(1, groups):
        other = lax.rem(g + k, groups)
        signal(at_z(2 * other))
        signal(at_z(2 * other + 1))

    tok = tokens_ref[...].astype(F32)
    stage32[...] = jnp.zeros_like(stage32)
    for k in range(SLICES * qn):
        stage32[4 * k : 4 * k + own_rows, :] = tok[:, 128 * k : 128 * (k + 1)]
    stage[...] = stage32[...].astype(BF).reshape(stage.shape)

    ids = ids_ref[...]
    gates = gates_ref[...].astype(F32)
    shares = gates / jnp.sum(gates, axis=0, keepdims=True)
    rows = ids.shape[1]
    line = iota((8, rows), 0)
    cat = jnp.zeros((8, rows), F32)
    for k in range(groups):
        hit = ids == c * groups + k
        named = jnp.sum(jnp.where(hit, 1.0, 0.0), axis=0, keepdims=True)
        weight = jnp.sum(jnp.where(hit, shares, 0.0), axis=0, keepdims=True)
        cat = jnp.where(line == k, named, cat)
        cat = jnp.where(line == 4 + k, weight, cat)
    upper = jnp.where(iota((rows, rows), 0) < iota((rows, rows), 1), 1.0, 0.0)
    rank = dot32(cat.astype(BF), upper.astype(BF))
    base = (i * CAP + 1).astype(F32)
    table = jnp.where(line < 4, jnp.where(cat > 0.0, rank + base, 0.0), cat)
    tabs[i] = jnp.concatenate([table, jnp.zeros((8, 128 - rows), F32)], axis=1)
    a0r[i] = stage[i]

    pl.semaphore_wait(barrier, SLICES - 1 + cols - 1 + zn - 2)

    def slice_copy(j):
        return remote(stage.at[j], a0r.at[i], a0s.at[j], a0q.at[i], at_cube(j))

    def table_copy(j):
        return remote(tabs.at[i], tabs.at[i], tbs.at[j], tbq.at[i], at_cube(j))

    for k in range(1, SLICES):
        start(slice_copy(lax.rem(i + k, SLICES)))
    for k in range(1, SLICES):
        start(table_copy(lax.rem(i + k, SLICES)))
    for k in range(1, SLICES):
        j = lax.rem(i + k, SLICES)
        remote(stage.at[j], a0r.at[j], a0s.at[j], a0q.at[j], at_cube(j)).wait_recv()

    flat = a0r[...].reshape(SLICES * 16, 128)
    row = iota((block, SLICES * 16), 0)
    hrow = jnp.where(row >= half, 1, 0)
    rem = row - half * hrow
    dpr = quotient(rem, own_rows, half)
    tgt = dpr * 16 + hrow * 4 + (rem - own_rows * dpr)
    colk = iota((block, SLICES * 16), 1)

    def block_copy(k, t):
        return remote(blk.at[t], gath.at[t, c], a1s.at[t, k], a1q.at[t, c], at_column(k))

    for t in range(2):
        perm = jnp.where(colk == tgt + 8 * t, 1.0, 0.0).astype(BF)
        blk[t] = dot32(perm, flat).astype(BF)
        for k in range(1, cols):
            start(block_copy(lax.rem(c + k, cols), t))
        gath[t, c] = blk[t]

    for k in range(1, SLICES):
        j = lax.rem(i + k, SLICES)
        remote(tabs.at[j], tabs.at[j], tbs.at[j], tbq.at[j], at_cube(j)).wait_recv()
    flat_tabs = tabs[...].reshape(SLICES * 8, 128)

    lm = iota((128, lanes), 1)
    cm = quotient(lm, block, lanes)
    rm = lm - block * cm
    hm = jnp.where(rm >= half, 1, 0)
    rm = rm - half * hm
    dm = quotient(rm, own_rows, half)
    tm = own_rows * cm + (rm - own_rows * dm)
    spread = jnp.where(iota((128, lanes), 0) == tm, 1.0, 0.0)
    wide = jnp.dot(flat_tabs, spread, precision=HIGH, preferred_element_type=F32)
    wide = jnp.where((iota((SLICES * 8, lanes), 0) >> 3) == dm[0 : SLICES * 8], wide, 0.0)
    wide = jnp.sum(wide.reshape(SLICES, 8, lanes), axis=0)
    slot_id = (iota((slots, lanes), 0) + 1).astype(F32)
    for h in range(2):
        for k in range(groups):
            key = jnp.where(hm[0:1] == h, wide[k : k + 1], 0.0)
            pick[h, k * slots : (k + 1) * slots, :] = jnp.where(
                slot_id == key, 1.0, 0.0
            ).astype(BF)

    def make_mix():
        mn = cols * half
        rows_m = iota((mn, 128), 0)
        cr = quotient(rows_m, half, mn)
        rr = rows_m - half * cr
        dr = quotient(rr, own_rows, half)
        tr = own_rows * cr + (rr - own_rows * dr)
        spread_t = jnp.where(iota((mn, 128), 1) == tr, 1.0, 0.0)
        tall = jnp.dot(spread_t, jnp.transpose(flat_tabs), precision=HIGH, preferred_element_type=F32)
        lane_t = iota((mn, SLICES * 8), 1)
        tall = jnp.where((lane_t >> 3) == dr[:, 0 : SLICES * 8], tall, 0.0)
        lane_w = iota((mn, zn * slots), 1)
        lz = quotient(lane_w, slots, zn * slots)
        slot_w = (lane_w - slots * lz + 1).astype(F32)
        lg = lz >> 1
        mix = jnp.zeros((mn, zn * slots), F32)
        for k in range(groups):
            key = jnp.sum(jnp.where((lane_t & 7) == k, tall, 0.0), axis=1, keepdims=True)
            wgt = jnp.sum(jnp.where((lane_t & 7) == 4 + k, tall, 0.0), axis=1, keepdims=True)
            mix = jnp.where((lg == k) & (slot_w == key), wgt, mix)
        mixw[...] = mix.astype(BF)

    make_mix()

    def zmod(k):
        return lax.rem(z + k, zn)

    def out_copy(k, t):
        return remote(
            sel.at[t, lax.div(k, 2)], xb.at[t, p, zb, g], bzs.at[t, k], bzq.at[t, z], at_z(k)
        )

    def spot(k, pos, t):
        return xb.at[t, pos, lax.rem(k, 2), lax.div(k, 2)]

    def in_z(k, t):
        ref = spot(k, p, t)
        return remote(ref, ref, bzs.at[t, k], bzq.at[t, k], at_z(k))

    def relay_copy(k, t):
        ref = spot(k, p, t)
        return remote(ref, ref, brs.at[t], bzq.at[t, k], at_z(z_mate_z))

    def x_copy(k, pos, t):
        ref = spot(k, pos, t)
        return remote(ref, ref, bxs.at[t, k], bxq.at[t, k], x_mate)

    def c_copy(k, pos, which, t):
        ref = spot(k, pos, t)
        return remote(ref, ref, bcs.at[t, which * zn + k], bcq.at[t, which * zn + k], core_mate)

    if ring8:
        kr = 5 - 2 * zb
        order = [0, 1, 7, kr, 2, 6, 8 - kr, 4]
        leave = order[1:7]
    else:
        order = list(range(zn))
        leave = order[1:]

    def pass_on(k, t):
        start(x_copy(k, p, t))
        start(c_copy(k, p, 0, t))

    def dispatch(t):
        def wait_block(k, _):
            j = lax.rem(c + k, cols)
            remote(
                blk.at[t], gath.at[t, j], a1s.at[t, j], a1q.at[t, j], at_column(j)
            ).wait_recv()
            return 0

        lax.fori_loop(1, cols, wait_block, 0)
        tokens_all = gath[t].reshape(lanes, 128)
        for h in range(2):
            got = dot32(pick[h], tokens_all).astype(BF)
            sel[t, :, :, 128 * h : 128 * (h + 1)] = got.reshape(groups, slots, 128)
        for k in leave:
            start(out_copy(zmod(k), t))
        xb[t, p, zb, g] = sel[t, g]
        pass_on(z, t)

    def arrive(n, t):
        src = zmod(order[n])
        in_z(src, t).wait_recv()
        if ring8 and n == 3:
            start(relay_copy(src, t))
        pass_on(src, t)

    def project(pos, t, first=False):
        for b in range(2):
            off = pl.multiple_of((b * 4 + pos) * sw + t * hw, hw)
            part = xb[t, pos, b].reshape(groups * slots, hw)
            up = dot_rows(part, wu[:, pl.ds(off, hw)])
            gate = dot_rows(part, wg[:, pl.ds(off, hw)])
            if first and b == 0:
                acc[0] = gate
                acc[1] = up
            else:
                acc[0] += gate
                acc[1] += up

    pc = xl * 2 + (1 - core)
    pxc = (1 - xl) * 2 + (1 - core)

    def cross(n, t):
        src = zmod(order[n])
        x_copy(src, px, t).wait_recv()
        start(c_copy(src, px, 1, t))

    def wait_core(pos, which, t):
        for k in range(zn):
            c_copy(k, pos, which, t).wait_recv()

    early, mid = min(EARLY, zn), zn // 2
    dispatch(0)
    for n in range(1, early):
        arrive(n, 0)
    dispatch(1)
    for n in range(early, zn):
        arrive(n, 0)
    loads[0].wait()
    loads[1].wait()
    project(p, 0, True)
    for n in range(1, mid + 1):
        arrive(n, 1)
    for n in range(mid):
        cross(n, 0)
    wait_core(pc, 0, 0)
    project(pc, 0)
    for n in range(mid + 1, zn):
        arrive(n, 1)
    for n in range(mid, zn):
        cross(n, 0)
    project(p, 1)
    project(px, 0)
    for n in range(mid):
        cross(n, 1)
    wait_core(pc, 0, 1)
    project(pc, 1)
    wait_core(pxc, 1, 0)
    project(pxc, 0)
    for n in range(mid, zn):
        cross(n, 1)
    project(px, 1)
    wait_core(pxc, 1, 1)
    project(pxc, 1)

    gate = acc[0]
    hid[...] = (gate / (1.0 + jnp.exp(-gate)) * acc[1]).astype(BF)
    loads[2].wait()

    def down(b, pos, t):
        off = pl.multiple_of((b * 4 + pos) * sw + t * hw, hw)
        return dot32(hid[...], wd[:, pl.ds(off, hw)]).reshape(groups, slots, hw)

    def pc_copy(which, b, t):
        n = 4 * which + 2 * t + b
        return remote(pcs.at[which, t, b], pcr.at[which, t, b], dcs.at[n], dcq.at[n], core_mate)

    def xd_copy(k, t):
        b, e = lax.rem(k, 2), lax.div(k, 2)
        return remote(xs.at[t, b, e], xr.at[t, b, e], dxs.at[t, k], dxq.at[t, k], x_mate)

    if ring8:
        back = [4, 8 - kr, kr, 2, 6, 1, 7, 0]
    else:
        back = list(range(zn - 1, -1, -1))
    for t in range(2):
        for b in range(2):
            pcs[0, t, b] = down(b, pxc, t).astype(BF)
            start(pc_copy(0, b, t))
    for t in range(2):
        for b in range(2):
            mine = down(b, px, t)
            pc_copy(0, b, t).wait_recv()
            xs[t, b] = (mine + pcr[0, t, b].astype(F32)).astype(BF)
        for k in back:
            start(xd_copy(zmod(k), t))
    for t in range(2):
        for b in range(2):
            pcs[1, t, b] = down(b, pc, t).astype(BF)
            start(pc_copy(1, b, t))
    for t in range(2):
        for b in range(2):
            mine = down(b, p, t)
            pc_copy(1, b, t).wait_recv()
            own[t, b] = mine + pcr[1, t, b].astype(F32)

    def home_copy(k, t):
        return remote(zs.at[t, k], zr.at[t, z], dzs.at[t, k], dzq.at[t, z], at_z(k))

    def lent_copy(t):
        return remote(rls.at[t], rl.at[t], rss.at[t], rsq.at[t], at_z(z_mate_z))

    def give_back(n, t):
        dst = zmod(back[n])
        b, e = lax.rem(dst, 2), lax.div(dst, 2)
        xd_copy(dst, t).wait_recv()
        total = own[t, b, e] + xr[t, b, e].astype(F32)
        if n == zn - 1:
            zr[t, z] = total.astype(BF)
        elif ring8 and n == 0:
            rls[t] = total.astype(BF)
            start(lent_copy(t))
        else:
            if ring8 and n == 2:
                lent_copy(t).wait_recv()
                total = total + rl[t].astype(F32)
            zs[t, dst] = total.astype(BF)
            start(home_copy(dst, t))

    def sum_copy(k, t):
        return remote(es.at[t, k], er.at[t, c], e1s.at[t, k], e1q.at[t, c], at_column(k))

    def settle(t):
        if ring8:
            zr[t, zmod(4)] = jnp.zeros((slots, hw), BF)
        for n, k in enumerate(back[:-1]):
            if ring8 and n == 0:
                continue
            src = zmod(zn - k)
            remote(
                zs.at[t, src], zr.at[t, src], dzs.at[t, src], dzq.at[t, src], at_z(src)
            ).wait_recv()
        mixed = dot32(mixw[...], zr[t].reshape(zn * slots, hw))
        for h in range(2):
            es32[:, half * h : half * (h + 1), :] = mixed[:, 128 * h : 128 * (h + 1)].reshape(
                cols, half, 128
            )
        es[t] = es32[...].astype(BF)
        for k in range(1, cols):
            start(sum_copy(lax.rem(c + k, cols), t))
        er[t, c] = es[t, c]

    for n in range(zn):
        give_back(n, 0)
    late = LATE if ring8 else zn - 1
    for n in range(late):
        give_back(n, 1)
    settle(0)
    for n in range(late, zn):
        give_back(n, 1)
    settle(1)
    finish(cols - 1)

    def column_sum(t):
        def wait_sum(k, _):
            j = lax.rem(c + k, cols)
            remote(
                es.at[t, j], er.at[t, j], e1s.at[t, j], e1q.at[t, j], at_column(j)
            ).wait_recv()
            return 0

        lax.fori_loop(1, cols, wait_sum, 0)
        total = er[t, 0].astype(F32)
        for k in range(1, cols):
            total = total + er[t, k].astype(F32)
        return total.astype(BF)

    colb = iota((SLICES * 16, block), 1)
    hcol = jnp.where(colb >= half, 1, 0)
    rem = colb - half * hcol
    dpc = quotient(rem, own_rows, half)
    tgt = dpc * 16 + hcol * 4 + (rem - own_rows * dpc)
    rowk = iota((SLICES * 16, block), 0)
    tiles = jnp.zeros((SLICES * 16, 128), F32)
    for t in range(2):
        perm = jnp.where(rowk == tgt + 8 * t, 1.0, 0.0).astype(BF)
        tiles = tiles + dot32(perm, column_sum(t))
    fin[...] = tiles.astype(BF).reshape(fin.shape)
    finr[i] = fin[i]

    for k in range(1, SLICES):
        j = lax.rem(i + k, SLICES)
        start(remote(fin.at[j], finr.at[i], e2s.at[j], e2q.at[i], at_cube(j)))
    for k in range(1, SLICES):
        j = lax.rem(i + k, SLICES)
        remote(fin.at[j], finr.at[j], e2s.at[j], e2q.at[j], at_cube(j)).wait_recv()
    stage32[...] = finr[...].astype(F32).reshape(SLICES * 16, 128)
    out_ref[...] = jnp.concatenate(
        [stage32[4 * k : 4 * k + own_rows, :] for k in range(SLICES * qn)], axis=1
    ).astype(BF)

    finish()


def local(tokens, expert_ids, gate_ints, gate_weight, up_weight, down_weight):
    groups = lax.axis_size("dp") // SLICES
    cols = lax.axis_size("expert")
    own_rows, width = tokens.shape
    hidden = gate_weight.shape[1]
    zn = 2 * groups
    sw = width // SLICES
    hw = sw // 2
    block = 2 * SLICES * own_rows
    half = SLICES * own_rows
    slots = SLICES * CAP
    vmem = pltpu.VMEM
    dma = pltpu.SemaphoreType.DMA
    sizes = (cols, groups, own_rows, width, hidden)
    scratch = [
        vmem((hidden, width), BF),
        vmem((hidden, width), BF),
        vmem((hidden, width), BF),
        vmem((SLICES * 16, 128), F32),
        vmem((SLICES, 16, 128), BF),
        vmem((SLICES, 16, 128), BF),
        vmem((SLICES, 8, 128), F32),
        vmem((2, block, 128), BF),
        vmem((2, cols, block, 128), BF),
        vmem((2, groups * slots, cols * block), BF),
        vmem((2, groups, slots, hw), BF),
        vmem((2, 4, 2, groups, slots, hw), BF),
        vmem((2, groups * slots, hidden), F32),
        vmem((groups * slots, hidden), BF),
        vmem((2, 2, 2, groups, slots, hw), BF),
        vmem((2, 2, 2, groups, slots, hw), BF),
        vmem((2, 2, groups, slots, hw), BF),
        vmem((2, 2, groups, slots, hw), BF),
        vmem((2, 2, groups, slots, hw), F32),
        vmem((2, zn, slots, hw), BF),
        vmem((2, zn, slots, hw), BF),
        vmem((2, slots, hw), BF),
        vmem((2, slots, hw), BF),
        vmem((cols * half, zn * slots), BF),
        vmem((cols, block, 128), F32),
        vmem((2, cols, block, 128), BF),
        vmem((2, cols, block, 128), BF),
        vmem((SLICES, 16, 128), BF),
        vmem((SLICES, 16, 128), BF),
        dma((3,)),
        dma((SLICES,)), dma((SLICES,)), dma((SLICES,)), dma((SLICES,)),
        dma((2, cols)), dma((2, cols)),
        dma((2, zn)), dma((2, zn)), dma((2,)),
        dma((2, zn)), dma((2, zn)), dma((2, 2 * zn)), dma((2, 2 * zn)),
        dma((8,)), dma((8,)), dma((2, zn)), dma((2, zn)),
        dma((2, zn)), dma((2, zn)), dma((2,)), dma((2,)),
        dma((2, cols)), dma((2, cols)), dma((SLICES,)), dma((SLICES,)),
    ]
    return pl.pallas_call(
        functools.partial(kernel, sizes),
        out_shape=jax.ShapeDtypeStruct((own_rows, width), BF),
        in_specs=[pl.BlockSpec(memory_space=pltpu.VMEM)] * 3
        + [pl.BlockSpec(memory_space=pl.ANY)] * 3,
        out_specs=pl.BlockSpec(memory_space=pltpu.VMEM),
        scratch_shapes=scratch,
        compiler_params=pltpu.CompilerParams(
            collective_id=0, has_side_effects=True, vmem_limit_bytes=56 * 1024 * 1024
        ),
    )(tokens, expert_ids.T, gate_ints.T, gate_weight, up_weight, down_weight)


def solution(mesh):
    return jax.shard_map(
        local,
        mesh=mesh,
        in_specs=(
            P(("dp", "expert"), None),
            P("dp", None),
            P("dp", None),
            P(("expert", "dp"), None, None),
            P(("expert", "dp"), None, None),
            P(("expert", "dp"), None, None),
        ),
        out_specs=P(("dp", "expert"), None),
        check_vma=False,
    )
```
